32 devices in a mesh: dom: 32 (over z, y, x, core).
Axes of the slice: x: 2, y: 2, z: 4, core: 2. Of those that a mesh axis runs over, the one named last changes fastest.
Arguments:
- coefficients: float32 [32, 27, 3, 3, 8, 128], P('dom'), may hold values from -11 to 11
- sketch: float32 [32, 3, 64, 8, 128], P('dom'), may hold values from -10 to 10
Outputs:
- basis_out: float32 [32, 3, 64, 8, 128], P('dom')
- factor: float32 [64, 64], replicated
The draws below stay inside these ranges and needn't reach their ends.
All inputs are finite; a program needn't handle non-finite values.
Results may differ from the reference program's by a relative error of at most 0.0003.
Values sent between devices are 32-bit elements; how exact they have to be, the bound alone decides.
No kernel may reach another device: no remote copies, remote signals or barrier semaphores. Data moves between devices by JAX's collectives and lax.ppermute only.
A program may use at most 64 MiB of HBM per device.

```python
import math
import jax
import jax.numpy as jnp
from jax import lax

NY = 8
NZ = 128
K = 64
NX = 32


def draw_coefficients(key, part):
    first_key = jax.random.fold_in(key, 11)
    second_key = jax.random.fold_in(key, 12)
    shape_all = (NX, 27, 3, 3, NY, NZ)
    base_values = jnp.clip(jax.random.normal(first_key, shape_all, jnp.float32), -4.0, 4.0)
    spread = math.log(10.0)
    row_scale = jnp.exp(jax.random.uniform(second_key, (NX, 1, 3, 1, NY, NZ), jnp.float32) * spread)
    return (base_values * row_scale / 9.0).astype(jnp.float32)


def draw_sketch(key, part):
    first_key = jax.random.fold_in(key, 21)
    second_key = jax.random.fold_in(key, 22)
    own_part = jnp.clip(jax.random.normal(first_key, (NX, 3, K, NY, NZ), jnp.float32), -4.0, 4.0)
    shared_part = jnp.clip(jax.random.normal(second_key, (NX, 3, 1, NY, NZ), jnp.float32), -4.0, 4.0)
    shared_weight = 0.8
    mixed = own_part + 0.6 * jnp.roll(own_part, 1, axis=2) + shared_weight * shared_part
    return mixed.astype(jnp.float32)


def setup_inputs(seed: int = 0) -> dict:
    key_list = jax.random.split(jax.random.key(seed), 3)
    return {
        "coefficients": draw_coefficients(jax.random.fold_in(key_list[2], 71), 0),
        "sketch": draw_sketch(jax.random.fold_in(key_list[2], 71), 0),
    }


def apply_blocks(padded, coefficients):
    planes = coefficients.shape[0]
    rows_y = coefficients.shape[4]
    cols_z = coefficients.shape[5]
    accum = jnp.zeros((planes, 3, padded.shape[2], rows_y, cols_z), jnp.float32)
    for shift_x in range(3):
        for shift_y in range(3):
            for shift_z in range(3):
                offset_index = shift_x * 9 + shift_y * 3 + shift_z
                window = padded[shift_x:shift_x + planes, :, :, shift_y:shift_y + rows_y, shift_z:shift_z + cols_z]
                for source in range(3):
                    accum = accum + coefficients[:, offset_index, :, source][:, :, None] * window[:, source][:, None]
    return accum

def upper_factor(gram_matrix):
    order = gram_matrix.shape[0]
    positions = jnp.arange(order, dtype=jnp.int32)

    def column_step(column, lower):
        row_part = lax.dynamic_index_in_dim(lower, column, 0, keepdims=False)
        target = lax.dynamic_index_in_dim(gram_matrix, column, 1, keepdims=False)
        remain = target - jnp.dot(lower, row_part, precision=lax.Precision.HIGHEST, preferred_element_type=jnp.float32)
        pivot = jnp.sqrt(lax.dynamic_index_in_dim(remain, column, 0, keepdims=False))
        new_column = jnp.where(positions >= column, remain / pivot, jnp.zeros_like(remain))
        return lax.dynamic_update_index_in_dim(lower, new_column, column, 1)
    lower = lax.fori_loop(0, order, column_step, jnp.zeros_like(gram_matrix))
    return lower.T

def upper_inverse(upper_part):
    order = upper_part.shape[0]
    identity = jnp.eye(order, dtype=upper_part.dtype)

    def row_step(count, solved):
        row = order - 1 - count
        upper_row = lax.dynamic_index_in_dim(upper_part, row, 0, keepdims=False)
        unit_row = lax.dynamic_index_in_dim(identity, row, 0, keepdims=False)
        pivot = lax.dynamic_index_in_dim(upper_row, row, 0, keepdims=False)
        known = jnp.dot(upper_row, solved, precision=lax.Precision.HIGHEST, preferred_element_type=jnp.float32)
        return lax.dynamic_update_index_in_dim(solved, (unit_row - known) / pivot, row, 0)
    return lax.fori_loop(0, order, row_step, jnp.zeros_like(upper_part))

def reference(coefficients, sketch):
    padded = jnp.pad(sketch, ((1, 1), (0, 0), (0, 0), (1, 1), (1, 1)))

    def one_plane(position):
        window = lax.dynamic_slice_in_dim(padded, position, 3, 0)
        coef_plane = lax.dynamic_slice_in_dim(coefficients, position, 1, 0)
        return apply_blocks(window, coef_plane)[0]
    applied = lax.map(one_plane, jnp.arange(NX, dtype=jnp.int32))
    gram_total = jnp.einsum('xakyz,xalyz->kl', applied, applied, precision=lax.Precision.HIGHEST) / (3.0 * NX * NY * NZ)
    factor = upper_factor(gram_total)
    inverse = upper_inverse(factor)
    basis_out = jnp.einsum('xalyz,lk->xakyz', applied, inverse, precision=lax.Precision.HIGHEST)
    return (basis_out, factor)
```

```python
import jax
import jax.numpy as jnp
from jax import lax
from jax.experimental import pallas as pl
from jax.experimental.pallas import tpu as pltpu
from jax.sharding import PartitionSpec as P

GROUP = 4
VMEM_LIMIT = 48 * 1024 * 1024


def iota(shape, dim):
    return lax.broadcasted_iota(jnp.int32, shape, dim)


def side_bases():
    odd = lax.axis_index("dom") % 2
    return (1 - odd) * 18, odd * 18


def prepare(coef_ref, out_ref, base, first, keep):
    rows_y, cols_z = coef_ref.shape[3:]
    sub = iota((rows_y, cols_z), 0)
    lane = iota((rows_y, cols_z), 1)
    for dy in range(3):
        for dz in range(3):
            valid = None
            if dy == 0:
                valid = sub < rows_y - 1
            elif dy == 2:
                valid = sub > 0
            edge = None
            if dz == 0:
                edge = lane > 0
            elif dz == 2:
                edge = lane < cols_z - 1
            for a in range(3):
                for b in range(3):
                    block = coef_ref[base + dy * 3 + dz, a, b]
                    if dy == 0:
                        block = pltpu.roll(block, rows_y - 1, 0)
                    elif dy == 2:
                        block = pltpu.roll(block, 1, 0)
                    mask = valid
                    if edge is not None:
                        mask = edge if mask is None else mask & edge
                    if keep is not None:
                        mask = keep if mask is None else mask & keep
                    if mask is not None:
                        block = jnp.where(mask, block, 0.0)
                    out_ref[first + dy * 3 + dz, a, b] = block


def contract(coef_ref, planes, start, acc_init):
    rows_y, cols_z = coef_ref.shape[3:]
    zero = jnp.zeros((GROUP, rows_y, cols_z), jnp.float32)
    acc = [[zero for _ in range(3)] for _ in range(3)]
    for sketch_ref, first in planes:
        for b in range(3):
            own = sketch_ref[b, pl.ds(start, GROUP)]
            for dz in range(3):
                moved = own
                if dz == 0:
                    moved = pltpu.roll(own, 1, 2)
                elif dz == 2:
                    moved = pltpu.roll(own, cols_z - 1, 2)
                for dy in range(3):
                    for a in range(3):
                        acc[dy][a] += coef_ref[first + dy * 3 + dz, a, b][None] * moved
    out = []
    for a in range(3):
        total = acc[1][a] + pltpu.roll(acc[0][a], 1, 1) + pltpu.roll(acc[2][a], rows_y - 1, 1)
        if acc_init is not None:
            total = total + acc_init(a)
        out.append(total)
    return out


def near_kernel(coef_ref, own_ref, pair_ref, part_ref, far_coef_ref, work):
    pair_base, chain_base = side_bases()
    me = lax.axis_index("dom")
    count = lax.axis_size("dom")
    lone = (me == 0) | (me == count - 1)
    rows_y, cols_z = coef_ref.shape[3:]
    keep = iota((rows_y, cols_z), 0) >= jnp.where(lone, rows_y, 0)
    prepare(coef_ref, work, 9, 0, None)
    prepare(coef_ref, work, pair_base, 9, None)
    prepare(coef_ref, far_coef_ref, chain_base, 0, keep)

    def step(i, carry):
        start = i * GROUP
        out = contract(work, [(own_ref, 0), (pair_ref, 9)], start, None)
        for a in range(3):
            part_ref[a, pl.ds(start, GROUP)] = out[a]
        return carry

    lax.fori_loop(0, own_ref.shape[1] // GROUP, step, 0)


def far_kernel(far_coef_ref, chain_ref, part_ref, split_ref, gram_ref, work):
    columns = chain_ref.shape[1]
    rows_y, cols_z = chain_ref.shape[2:]

    def step(i, carry):
        start = i * GROUP
        out = contract(
            far_coef_ref, [(chain_ref, 0)], start, lambda a: part_ref[a, pl.ds(start, GROUP)]
        )
        for a in range(3):
            work[a, pl.ds(start * rows_y, GROUP * rows_y)] = out[a].reshape(GROUP * rows_y, cols_z)
        return carry

    lax.fori_loop(0, columns // GROUP, step, 0)
    total = jnp.zeros((2 * columns, 2 * columns), jnp.float32)
    for a in range(3):
        for y in range(0, rows_y, 2):
            both = []
            for yy in (y, y + 1):
                x = work[a, pl.ds(yy, columns, stride=rows_y)]
                high = x.astype(jnp.bfloat16)
                low = (x - high.astype(jnp.float32)).astype(jnp.bfloat16)
                stack = jnp.concatenate([high, low], axis=0)
                both.append(stack)
            wide = jnp.concatenate(both, axis=1)
            split_ref[(a * rows_y + y) // 2] = wide
            total += lax.dot_general(
                wide, wide, (((1,), (1,)), ((), ())), preferred_element_type=jnp.float32
            )
    rows = total[:columns] + total[columns:]
    gram = rows + pltpu.roll(rows, columns, 1)
    half = columns // 2
    lane = iota((half, 2 * columns), 1)
    gram_ref[...] = jnp.where(lane < columns, gram[:half], gram[half:])


def factor_rows(gram, columns):
    half = columns // 2
    lane = iota((half, 2 * columns), 1)
    sub = iota((half, 2 * columns), 0)
    top = jnp.where(lane < columns, gram, jnp.where(lane - columns == sub, 1.0, 0.0))
    low = jnp.where(
        lane < columns,
        pltpu.roll(gram, columns, 1),
        jnp.where(lane - columns == sub + half, 1.0, 0.0),
    )
    count = columns // 8
    shape = (8, 2 * columns)
    blocks = [top[8 * j : 8 * j + 8] for j in range(count // 2)]
    blocks += [low[8 * j : 8 * j + 8] for j in range(count // 2)]
    sub8 = iota(shape, 0)
    done = []
    for j in range(count):
        panel = [
            [
                jnp.broadcast_to(blocks[r][:, 8 * j + c : 8 * j + c + 1], shape)
                for c in range(8)
            ]
            for r in range(j, count)
        ]
        live = blocks[j:]
        pivots = jnp.ones(shape, jnp.float32)
        for i in range(8):
            row = jnp.broadcast_to(live[0][i : i + 1], shape)
            heads = {
                c: jnp.broadcast_to(panel[0][c][i : i + 1], shape) for c in range(i, 8)
            }
            inverse = 1.0 / heads[i]
            pivots = jnp.where(sub8 == i, heads[i], pivots)
            for r in range(count - j):
                scale = panel[r][i] * inverse
                if r == 0:
                    if i == 7:
                        continue
                    scale = jnp.where(sub8 > i, scale, 0.0)
                for c in range(i + 1, 8):
                    panel[r][c] = panel[r][c] - scale * heads[c]
                live[r] = live[r] - scale * row
        blocks[j + 1 :] = live[1:]
        done.append(live[0] * (1.0 / jnp.sqrt(pivots)))
    return jnp.concatenate(done, axis=0)


def basis_kernel(gram_ref, split_ref, basis_ref, factor_ref, *, scale):
    half, width = gram_ref.shape
    columns = 2 * half
    scaled = factor_rows(gram_ref[...] / scale, columns)
    lane = iota((columns, width), 1)
    sub = iota((columns, width), 0)
    factor_ref[...] = jnp.where(lane >= sub, scaled, 0.0)[:, :columns]
    right = jnp.where(lane >= columns, scaled, 0.0)
    twice = right + pltpu.roll(right, columns, 1)
    high = twice.astype(jnp.bfloat16)
    low = (twice - high.astype(jnp.float32)).astype(jnp.bfloat16)
    left = jnp.concatenate([high, low], axis=0)
    rows_y = basis_ref.shape[1] // columns
    cols_z = basis_ref.shape[2]
    for a in range(3):
        for y in range(0, rows_y, 2):
            wide = jnp.dot(
                left, split_ref[(a * rows_y + y) // 2], preferred_element_type=jnp.float32
            )
            wide = wide[:columns] + wide[columns:]
            for k in range(2):
                basis_ref[a, pl.ds(y + k, columns, stride=rows_y)] = wide[
                    :, k * cols_z : (k + 1) * cols_z
                ]


def vmem(count):
    return [pl.BlockSpec(memory_space=pltpu.VMEM)] * count


def params():
    return pltpu.CompilerParams(vmem_limit_bytes=VMEM_LIMIT)


def sum_over_devices(x):
    count = lax.axis_size("dom")
    bit = 1
    while bit < count:
        if bit == 1 or bit * 2 >= count:
            masks = [bit]
        else:
            masks = [bit, 2 * bit, 3 * bit]
        parts = [
            lax.ppermute(x, "dom", [(i, i ^ m) for i in range(count)]) for m in masks
        ]
        for part in parts:
            x = x + part
        bit *= len(masks) + 1
    return x


def shards(coefficients, sketch):
    count = lax.axis_size("dom")
    coefs = coefficients[0]
    own = sketch[0]
    _, columns, rows_y, cols_z = own.shape
    chain = [(i, (i + 1) % count) for i in range(1, count, 2)]
    chain += [(b, a) for a, b in chain]
    chain_plane = lax.ppermute(own, "dom", chain)
    pair_plane = lax.ppermute(own, "dom", [(i, i ^ 1) for i in range(count)])
    part, far_coefs = pl.pallas_call(
        near_kernel,
        out_shape=(
            jax.ShapeDtypeStruct(own.shape, jnp.float32),
            jax.ShapeDtypeStruct((9, 3, 3, rows_y, cols_z), jnp.float32),
        ),
        in_specs=vmem(3),
        out_specs=tuple(vmem(2)),
        scratch_shapes=[pltpu.VMEM((18, 3, 3, rows_y, cols_z), jnp.float32)],
        compiler_params=params(),
        cost_estimate=pl.CostEstimate(
            flops=2 * 162 * own.size // 3, bytes_accessed=4 * own.size * 5, transcendentals=0
        ),
        name="near",
    )(coefs, own, pair_plane)
    split, gram = pl.pallas_call(
        far_kernel,
        out_shape=(
            jax.ShapeDtypeStruct((3 * rows_y // 2, 2 * columns, 2 * cols_z), jnp.bfloat16),
            jax.ShapeDtypeStruct((columns // 2, 2 * columns), jnp.float32),
        ),
        in_specs=vmem(3),
        out_specs=tuple(vmem(2)),
        scratch_shapes=[pltpu.VMEM((3, columns * rows_y, cols_z), jnp.float32)],
        compiler_params=params(),
        name="far",
    )(far_coefs, chain_plane, part)
    gram = sum_over_devices(gram)
    scale = 3.0 * count * rows_y * cols_z
    basis, factor = pl.pallas_call(
        lambda *refs: basis_kernel(*refs, scale=scale),
        out_shape=(
            jax.ShapeDtypeStruct((3, columns * rows_y, cols_z), jnp.float32),
            jax.ShapeDtypeStruct((columns, columns), jnp.float32),
        ),
        in_specs=vmem(2),
        out_specs=tuple(vmem(2)),
        compiler_params=params(),
        name="basis",
    )(gram, split)
    return basis.reshape(sketch.shape), factor


def solution(mesh):
    placed = (P("dom", None, None, None, None, None), P("dom", None, None, None, None))
    return jax.shard_map(
        shards,
        mesh=mesh,
        in_specs=placed,
        out_specs=(P("dom", None, None, None, None), P()),
        check_vma=False,
    )
```

```python
import functools

import jax
import jax.numpy as jnp
from jax import lax
from jax.experimental import pallas as pl
from jax.experimental.pallas import tpu as pltpu
from jax.sharding import PartitionSpec as P

GROUP = 4
VMEM_LIMIT = 48 * 1024 * 1024


def iota(shape, dim):
    return lax.broadcasted_iota(jnp.int32, shape, dim)


def side_bases():
    odd = lax.axis_index("dom") % 2
    return (1 - odd) * 18, odd * 18


def prepare(coef_ref, out_ref, base, first, keep):
    rows_y, cols_z = coef_ref.shape[3:]
    sub = iota((rows_y, cols_z), 0)
    lane = iota((rows_y, cols_z), 1)
    for dy in range(3):
        for dz in range(3):
            valid = None
            if dy == 0:
                valid = sub < rows_y - 1
            elif dy == 2:
                valid = sub > 0
            edge = None
            if dz == 0:
                edge = lane > 0
            elif dz == 2:
                edge = lane < cols_z - 1
            for a in range(3):
                for b in range(3):
                    block = coef_ref[base + dy * 3 + dz, a, b]
                    if dy == 0:
                        block = pltpu.roll(block, rows_y - 1, 0)
                    elif dy == 2:
                        block = pltpu.roll(block, 1, 0)
                    mask = valid
                    if edge is not None:
                        mask = edge if mask is None else mask & edge
                    if keep is not None:
                        mask = keep if mask is None else mask & keep
                    if mask is not None:
                        block = jnp.where(mask, block, 0.0)
                    out_ref[first + dy * 3 + dz, a, b] = block


def contract(coef_ref, parts, start, initial):
    rows_y, cols_z = coef_ref.shape[3:]
    zero = jnp.zeros((GROUP, rows_y, cols_z), jnp.float32)
    acc = [[zero for _ in range(3)] for _ in range(3)]
    for sketch_ref, slot, b, first in parts:
        own = sketch_ref[slot, pl.ds(start, GROUP)]
        for dz in range(3):
            moved = own
            if dz == 0:
                moved = pltpu.roll(own, 1, 2)
            elif dz == 2:
                moved = pltpu.roll(own, cols_z - 1, 2)
            for dy in range(3):
                for a in range(3):
                    acc[dy][a] += coef_ref[first + dy * 3 + dz, a, b][None] * moved
    out = []
    for a in range(3):
        total = acc[1][a] + pltpu.roll(acc[0][a], 1, 1) + pltpu.roll(acc[2][a], rows_y - 1, 1)
        if initial is not None:
            total = total + initial[a, pl.ds(start, GROUP)]
        out.append(total)
    return out


def near_kernel(coef_ref, own_ref, pair_ref, part_ref, far_coef_ref, work):
    pair_base, chain_base = side_bases()
    me = lax.axis_index("dom")
    count = lax.axis_size("dom")
    lone = (me == 0) | (me == count - 1)
    rows_y, cols_z = coef_ref.shape[3:]
    keep = iota((rows_y, cols_z), 0) >= jnp.where(lone, rows_y, 0)
    prepare(coef_ref, work, 9, 0, None)
    prepare(coef_ref, work, pair_base, 9, None)
    prepare(coef_ref, far_coef_ref, chain_base, 0, keep)
    parts = [(own_ref, b, b, 0) for b in range(3)] + [(pair_ref, b, b, 9) for b in range(3)]

    def step(i, carry):
        start = i * GROUP
        out = contract(work, parts, start, None)
        for a in range(3):
            part_ref[a, pl.ds(start, GROUP)] = out[a]
        return carry

    lax.fori_loop(0, own_ref.shape[1] // GROUP, step, 0)


def middle_kernel(far_coef_ref, chain_ref, part_ref, out_ref, *, component):
    def step(i, carry):
        start = i * GROUP
        out = contract(far_coef_ref, [(chain_ref, 0, component, 0)], start, part_ref)
        for a in range(3):
            out_ref[a, pl.ds(start, GROUP)] = out[a]
        return carry

    lax.fori_loop(0, chain_ref.shape[1] // GROUP, step, 0)


def pack(gram, half, columns):
    quarter = columns // 4
    width = 2 * columns
    lane = iota((quarter, width), 1) % columns
    sub = iota((quarter, width), 0)
    base = half * 2 * quarter
    first = pltpu.roll(gram[base : base + quarter], (width - base) % width, 1)
    second = pltpu.roll(gram[base + quarter : base + 2 * quarter], width - base - quarter, 1)
    cross = gram[half * quarter : (half + 1) * quarter]
    packed = jnp.where(
        (lane < quarter) & (lane < sub), second, jnp.where(lane < 2 * quarter, first, cross)
    )
    last = jnp.sum(jnp.where(lane == sub, second, 0.0), axis=0, keepdims=True)
    wide = iota((8, width), 1)
    return [jnp.where(wide < columns, packed[:8], packed[8:]), last]


def last_kernel(
    far_coef_ref, chain_ref, part_ref, split_ref, mine_ref, twin_ref, work, *, component
):
    columns = chain_ref.shape[1]
    rows_y, cols_z = chain_ref.shape[2:]

    def step(i, carry):
        start = i * GROUP
        out = contract(far_coef_ref, [(chain_ref, 0, component, 0)], start, part_ref)
        for a in range(3):
            for k in range(GROUP):
                work[a, pl.ds(start + k, rows_y, stride=columns)] = out[a][k]
        return carry

    lax.fori_loop(0, columns // GROUP, step, 0)
    total = jnp.zeros((2 * columns, 2 * columns), jnp.float32)
    for a in range(3):
        for y in range(0, rows_y, 2):
            both = []
            for yy in (y, y + 1):
                x = work[a, pl.ds(yy * columns, columns)]
                high = x.astype(jnp.bfloat16)
                low = (x - high.astype(jnp.float32)).astype(jnp.bfloat16)
                both.append(jnp.concatenate([high, low], axis=0))
            wide = jnp.concatenate(both, axis=1)
            split_ref[(a * rows_y + y) // 2] = wide
            total += lax.dot_general(
                wide, wide, (((1,), (1,)), ((), ())), preferred_element_type=jnp.float32
            )
    rows = total[:columns] + total[columns:]
    gram = rows + pltpu.roll(rows, columns, 1)
    odd = lax.axis_index("dom") % 2 == 1
    halves = [pack(gram, h, columns) for h in range(2)]
    for ref, flip in ((mine_ref, False), (twin_ref, True)):
        low, high = halves[::-1] if flip else halves
        body = jnp.where(odd, high[0], low[0])
        for r in range(8):
            ref[:, r * 2 * columns : (r + 1) * 2 * columns] = body[r : r + 1]
        ref[:, 16 * columns :] = jnp.where(odd, high[1], low[1])


def unpack(parts_ref, columns):
    width = 2 * columns
    quarter = columns // 4
    sub8 = iota((8, width), 0)
    rows = []
    for r in range(9):
        x = parts_ref[:, 0, r * width : (r + 1) * width]
        x = jnp.sum(x.reshape(x.shape[0] // 8, 8, width), axis=0)
        x = x + pltpu.roll(x, 2, 0)
        rows.append(x + pltpu.roll(x, 4, 0))
    lane = iota((quarter, width), 1)
    sub = iota((quarter, width), 0)
    out = []
    for half in range(2):
        body = jnp.zeros((8, width), jnp.float32)
        for r in range(8):
            body = jnp.where(
                sub8 == r, jnp.broadcast_to(rows[r][half : half + 1], (8, width)), body
            )
        packed = jnp.concatenate([body, pltpu.roll(body, columns, 1)], axis=0)
        base = half * 2 * quarter
        upper = jnp.where(lane >= sub, packed, 0.0)
        upper = jnp.where(lane < 2 * quarter, upper, 0.0)
        lower = jnp.where(lane < sub, packed, 0.0)
        diag = jnp.broadcast_to(rows[8][half : half + 1], (quarter, width))
        lower = jnp.where(lane == sub, diag, lower)
        lower = jnp.where(lane < quarter, lower, 0.0)
        cross = jnp.where((lane >= 2 * quarter) & (lane < columns), packed, 0.0)
        if base:
            upper = pltpu.roll(upper, base, 1)
        out.append((upper, pltpu.roll(lower, base + quarter, 1), cross))
    once = jnp.concatenate(
        [out[0][0] + out[0][2], out[0][1] + out[1][2], out[1][0], out[1][1]], axis=0
    )
    lane = iota((columns, width), 1)
    sub = iota((columns, width), 0)
    square = jnp.concatenate([once, jnp.zeros_like(once)], axis=0)
    mirror = jnp.transpose(square)[:columns]
    return once + jnp.where(lane == sub, 0.0, mirror)


def factor_rows(gram, columns):
    lane = iota(gram.shape, 1)
    sub = iota(gram.shape, 0)
    both = jnp.where(lane - columns == sub, 1.0, gram)
    count = columns // 8
    shape = (8, 2 * columns)
    blocks = [both[8 * j : 8 * j + 8] for j in range(count)]
    sub8 = iota(shape, 0)
    done = []
    for j in range(count):
        panel = [
            [
                jnp.broadcast_to(blocks[r][:, 8 * j + c : 8 * j + c + 1], shape)
                for c in range(8)
            ]
            for r in range(j, count)
        ]
        live = blocks[j:]
        pivots = jnp.ones(shape, jnp.float32)
        for i in range(8):
            row = jnp.broadcast_to(live[0][i : i + 1], shape)
            heads = {
                c: jnp.broadcast_to(panel[0][c][i : i + 1], shape) for c in range(i, 8)
            }
            inverse = 1.0 / heads[i]
            pivots = jnp.where(sub8 == i, heads[i], pivots)
            for r in range(count - j):
                scale = panel[r][i] * inverse
                if r == 0:
                    if i == 7:
                        continue
                    scale = jnp.where(sub8 > i, scale, 0.0)
                for c in range(i + 1, 8):
                    panel[r][c] = panel[r][c] - scale * heads[c]
                live[r] = live[r] - scale * row
        blocks[j + 1 :] = live[1:]
        done.append(live[0] * (1.0 / jnp.sqrt(pivots)))
    return jnp.concatenate(done, axis=0)


def basis_kernel(parts_ref, split_ref, basis_ref, factor_ref, *, scale):
    columns = factor_ref.shape[0]
    width = 2 * columns
    scaled = factor_rows(unpack(parts_ref, columns) / scale, columns)
    lane = iota((columns, width), 1)
    sub = iota((columns, width), 0)
    factor_ref[...] = jnp.where(lane >= sub, scaled, 0.0)[:, :columns]
    right = jnp.where(lane >= columns, scaled, 0.0)
    twice = right + pltpu.roll(right, columns, 1)
    high = twice.astype(jnp.bfloat16)
    low = (twice - high.astype(jnp.float32)).astype(jnp.bfloat16)
    left = jnp.concatenate([high, low], axis=0)
    rows_y = basis_ref.shape[1] // columns
    cols_z = basis_ref.shape[2]
    for a in range(3):
        for y in range(0, rows_y, 2):
            wide = jnp.dot(
                left, split_ref[(a * rows_y + y) // 2], preferred_element_type=jnp.float32
            )
            wide = wide[:columns] + wide[columns:]
            for k in range(2):
                basis_ref[a, pl.ds(y + k, columns, stride=rows_y)] = wide[
                    :, k * cols_z : (k + 1) * cols_z
                ]


def vmem(count):
    return [pl.BlockSpec(memory_space=pltpu.VMEM)] * count


def params():
    return pltpu.CompilerParams(vmem_limit_bytes=VMEM_LIMIT)


def shards(coefficients, sketch):
    count = lax.axis_size("dom")
    coefs = coefficients[0]
    own = sketch[0]
    _, columns, rows_y, cols_z = own.shape
    chain = [(i, (i + 1) % count) for i in range(1, count, 2)]
    chain += [(b, a) for a, b in chain]
    faces = [lax.ppermute(own[b : b + 1], "dom", chain) for b in range(3)]
    pairs = [(i, i ^ 1) for i in range(count)]
    pair_plane = lax.ppermute(own, "dom", pairs)
    part, far_coefs = pl.pallas_call(
        near_kernel,
        out_shape=(
            jax.ShapeDtypeStruct(own.shape, jnp.float32),
            jax.ShapeDtypeStruct((9, 3, 3, rows_y, cols_z), jnp.float32),
        ),
        in_specs=vmem(3),
        out_specs=tuple(vmem(2)),
        scratch_shapes=[pltpu.VMEM((18, 3, 3, rows_y, cols_z), jnp.float32)],
        compiler_params=params(),
        cost_estimate=pl.CostEstimate(
            flops=2 * 162 * own.size // 3, bytes_accessed=4 * own.size * 5, transcendentals=0
        ),
        name="near",
    )(coefs, own, pair_plane)
    for b in range(2):
        part = pl.pallas_call(
            functools.partial(middle_kernel, component=b),
            out_shape=jax.ShapeDtypeStruct(own.shape, jnp.float32),
            in_specs=vmem(3),
            out_specs=vmem(1)[0],
            compiler_params=params(),
            name="middle",
        )(far_coefs, faces[b], part)
    packed = jax.ShapeDtypeStruct((1, 18 * columns), jnp.float32)
    split, mine, twin = pl.pallas_call(
        functools.partial(last_kernel, component=2),
        out_shape=(
            jax.ShapeDtypeStruct((3 * rows_y // 2, 2 * columns, 2 * cols_z), jnp.bfloat16),
            packed,
            packed,
        ),
        in_specs=vmem(3),
        out_specs=tuple(vmem(3)),
        scratch_shapes=[pltpu.VMEM((3, columns * rows_y, cols_z), jnp.float32)],
        compiler_params=params(),
        name="last",
    )(far_coefs, faces[2], part)
    mine = mine + lax.ppermute(twin, "dom", pairs)
    parts = lax.all_to_all(jnp.broadcast_to(mine, (count,) + mine.shape), "dom", 0, 0)
    scale = 3.0 * count * rows_y * cols_z
    basis, factor = pl.pallas_call(
        functools.partial(basis_kernel, scale=scale),
        out_shape=(
            jax.ShapeDtypeStruct((3, columns * rows_y, cols_z), jnp.float32),
            jax.ShapeDtypeStruct((columns, columns), jnp.float32),
        ),
        in_specs=vmem(2),
        out_specs=tuple(vmem(2)),
        compiler_params=params(),
        name="basis",
    )(parts, split)
    return basis.reshape(sketch.shape), factor


def solution(mesh):
    placed = (P("dom", None, None, None, None, None), P("dom", None, None, None, None))
    return jax.shard_map(
        shards,
        mesh=mesh,
        in_specs=placed,
        out_specs=(P("dom", None, None, None, None), P()),
        check_vma=False,
    )
```

```python
import functools

import jax
import jax.numpy as jnp
from jax import lax
from jax.experimental import pallas as pl
from jax.experimental.pallas import tpu as pltpu
from jax.sharding import PartitionSpec as P

GROUP = 4
UNROLL = 4
VMEM_LIMIT = 48 * 1024 * 1024


def iota(shape, dim):
    return lax.broadcasted_iota(jnp.int32, shape, dim)


def side_bases():
    odd = lax.axis_index("dom") % 2
    return (1 - odd) * 18, odd * 18


def prepare(coef_ref, out_ref, base, first, keep):
    rows_y, cols_z = coef_ref.shape[3:]
    sub = iota((rows_y, cols_z), 0)
    lane = iota((rows_y, cols_z), 1)
    for dy in range(3):
        for dz in range(3):
            valid = None
            if dy == 0:
                valid = sub < rows_y - 1
            elif dy == 2:
                valid = sub > 0
            edge = None
            if dz == 0:
                edge = lane > 0
            elif dz == 2:
                edge = lane < cols_z - 1
            for a in range(3):
                for b in range(3):
                    block = coef_ref[base + dy * 3 + dz, a, b]
                    if dy == 0:
                        block = pltpu.roll(block, rows_y - 1, 0)
                    elif dy == 2:
                        block = pltpu.roll(block, 1, 0)
                    mask = valid
                    if edge is not None:
                        mask = edge if mask is None else mask & edge
                    if keep is not None:
                        mask = keep if mask is None else mask & keep
                    if mask is not None:
                        block = jnp.where(mask, block, 0.0)
                    out_ref[first + dy * 3 + dz, a, b] = block


def contract(coef_ref, parts, start, initial):
    rows_y, cols_z = coef_ref.shape[3:]
    zero = jnp.zeros((GROUP, rows_y, cols_z), jnp.float32)
    acc = [[zero for _ in range(3)] for _ in range(3)]
    for sketch_ref, slot, b, first in parts:
        own = sketch_ref[slot, pl.ds(start, GROUP)]
        for dz in range(3):
            moved = own
            if dz == 0:
                moved = pltpu.roll(own, 1, 2)
            elif dz == 2:
                moved = pltpu.roll(own, cols_z - 1, 2)
            for dy in range(3):
                for a in range(3):
                    acc[dy][a] += coef_ref[first + dy * 3 + dz, a, b][None] * moved
    out = []
    for a in range(3):
        total = acc[1][a] + pltpu.roll(acc[0][a], 1, 1) + pltpu.roll(acc[2][a], rows_y - 1, 1)
        if initial is not None:
            total = total + initial[a, pl.ds(start, GROUP)]
        out.append(total)
    return out


def near_kernel(coef_ref, own_ref, pair_ref, part_ref, far_coef_ref, work):
    pair_base, chain_base = side_bases()
    me = lax.axis_index("dom")
    count = lax.axis_size("dom")
    lone = (me == 0) | (me == count - 1)
    rows_y, cols_z = coef_ref.shape[3:]
    keep = iota((rows_y, cols_z), 0) >= jnp.where(lone, rows_y, 0)
    prepare(coef_ref, work, 9, 0, None)
    prepare(coef_ref, work, pair_base, 9, None)
    prepare(coef_ref, far_coef_ref, chain_base, 0, keep)
    parts = [(own_ref, b, b, 0) for b in range(3)] + [(pair_ref, b, b, 9) for b in range(3)]

    def step(i, carry):
        start = i * GROUP
        out = contract(work, parts, start, None)
        for a in range(3):
            part_ref[a, pl.ds(start, GROUP)] = out[a]
        return carry

    lax.fori_loop(0, own_ref.shape[1] // GROUP, step, 0, unroll=UNROLL)


def pack(gram, half, columns):
    quarter = columns // 4
    width = 2 * columns
    lane = iota((quarter, width), 1) % columns
    sub = iota((quarter, width), 0)
    base = half * 2 * quarter
    first = pltpu.roll(gram[base : base + quarter], (width - base) % width, 1)
    second = pltpu.roll(gram[base + quarter : base + 2 * quarter], width - base - quarter, 1)
    cross = gram[half * quarter : (half + 1) * quarter]
    packed = jnp.where(
        (lane < quarter) & (lane < sub), second, jnp.where(lane < 2 * quarter, first, cross)
    )
    last = jnp.sum(jnp.where(lane == sub, second, 0.0), axis=0, keepdims=True)
    wide = iota((8, width), 1)
    return [jnp.where(wide < columns, packed[:8], packed[8:]), last]


def far_kernel(far_coef_ref, chain_ref, part_ref, split_ref, mine_ref, twin_ref, work):
    columns = chain_ref.shape[1]
    rows_y, cols_z = chain_ref.shape[2:]
    parts = [(chain_ref, b, b, 0) for b in range(3)]

    def step(i, carry):
        start = i * GROUP
        out = contract(far_coef_ref, parts, start, part_ref)
        for a in range(3):
            work[a, pl.ds(start * rows_y, GROUP * rows_y)] = out[a].reshape(
                GROUP * rows_y, cols_z
            )
        return carry

    lax.fori_loop(0, columns // GROUP, step, 0, unroll=UNROLL)
    total = jnp.zeros((2 * columns, 2 * columns), jnp.float32)
    for a in range(3):
        for y in range(0, rows_y, 2):
            both = []
            for yy in (y, y + 1):
                x = work[a, pl.ds(yy, columns, stride=rows_y)]
                high = x.astype(jnp.bfloat16)
                low = (x - high.astype(jnp.float32)).astype(jnp.bfloat16)
                both.append(jnp.concatenate([high, low], axis=0))
            wide = jnp.concatenate(both, axis=1)
            split_ref[(a * rows_y + y) // 2] = wide
            total += lax.dot_general(
                wide, wide, (((1,), (1,)), ((), ())), preferred_element_type=jnp.float32
            )
    rows = total[:columns] + total[columns:]
    gram = rows + pltpu.roll(rows, columns, 1)
    odd = lax.axis_index("dom") % 2 == 1
    halves = [pack(gram, h, columns) for h in range(2)]
    for ref, flip in ((mine_ref, False), (twin_ref, True)):
        low, high = halves[::-1] if flip else halves
        body = jnp.where(odd, high[0], low[0])
        for r in range(8):
            ref[:, r * 2 * columns : (r + 1) * 2 * columns] = body[r : r + 1]
        ref[:, 16 * columns :] = jnp.where(odd, high[1], low[1])


def unpack(parts_ref, columns):
    width = 2 * columns
    quarter = columns // 4
    sub8 = iota((8, width), 0)
    rows = []
    for r in range(9):
        x = parts_ref[:, 0, r * width : (r + 1) * width]
        x = jnp.sum(x.reshape(x.shape[0] // 8, 8, width), axis=0)
        x = x + pltpu.roll(x, 2, 0)
        rows.append(x + pltpu.roll(x, 4, 0))
    lane = iota((quarter, width), 1)
    sub = iota((quarter, width), 0)
    out = []
    for half in range(2):
        body = jnp.zeros((8, width), jnp.float32)
        for r in range(8):
            body = jnp.where(
                sub8 == r, jnp.broadcast_to(rows[r][half : half + 1], (8, width)), body
            )
        packed = jnp.concatenate([body, pltpu.roll(body, columns, 1)], axis=0)
        base = half * 2 * quarter
        upper = jnp.where(lane >= sub, packed, 0.0)
        upper = jnp.where(lane < 2 * quarter, upper, 0.0)
        lower = jnp.where(lane < sub, packed, 0.0)
        diag = jnp.broadcast_to(rows[8][half : half + 1], (quarter, width))
        lower = jnp.where(lane == sub, diag, lower)
        lower = jnp.where(lane < quarter, lower, 0.0)
        cross = jnp.where((lane >= 2 * quarter) & (lane < columns), packed, 0.0)
        if base:
            upper = pltpu.roll(upper, base, 1)
        out.append((upper, pltpu.roll(lower, base + quarter, 1), cross))
    once = jnp.concatenate(
        [out[0][0] + out[0][2], out[0][1] + out[1][2], out[1][0], out[1][1]], axis=0
    )
    lane = iota((columns, width), 1)
    sub = iota((columns, width), 0)
    square = jnp.concatenate([once, jnp.zeros_like(once)], axis=0)
    mirror = jnp.transpose(square)[:columns]
    return once + jnp.where(lane == sub, 0.0, mirror)


def factor_rows(gram, columns):
    lane = iota(gram.shape, 1)
    sub = iota(gram.shape, 0)
    both = jnp.where(lane - columns == sub, 1.0, gram)
    count = columns // 8
    shape = (8, 2 * columns)
    blocks = [both[8 * j : 8 * j + 8] for j in range(count)]
    sub8 = iota(shape, 0)
    def spread(block, column):
        return jnp.broadcast_to(block[:, column : column + 1], shape)

    def repeat(block, row):
        return jnp.broadcast_to(block[row : row + 1], shape)

    done = []
    ahead = [spread(blocks[0], c) for c in range(8)]
    for j in range(count):
        own = ahead
        mine = blocks[j]
        rest = range(j + 1, count)
        if j + 1 < count:
            ahead = [spread(blocks[j + 1], 8 * (j + 1) + c) for c in range(8)]
        panel = {r: [spread(blocks[r], 8 * j + c) for c in range(8)] for r in rest}
        pivots = None
        for i in range(8):
            heads = {c: repeat(own[c], i) for c in range(i, 8)}
            row = repeat(mine, i)
            inverse = 1.0 / heads[i]
            pivots = heads[i] if i == 0 else jnp.where(sub8 == i, heads[i], pivots)
            if i < 7:
                scale = jnp.where(sub8 > i, own[i] * inverse, 0.0)
                for c in range(i + 1, 8):
                    if c == i + 1:
                        product = jnp.where(sub8 > i, own[i] * heads[c], 0.0)
                        own[c] = own[c] - product * inverse
                    else:
                        own[c] = own[c] - scale * heads[c]
                mine = mine - scale * row
            for r in rest:
                scale = panel[r][i] * inverse
                if r == j + 1:
                    for c in range(8):
                        ahead[c] = ahead[c] - scale * repeat(panel[r][i], c)
                for c in range(i + 1, 8):
                    panel[r][c] = panel[r][c] - scale * heads[c]
                blocks[r] = blocks[r] - scale * row
        done.append(mine * (1.0 / jnp.sqrt(pivots)))
    return jnp.concatenate(done, axis=0)


def basis_kernel(parts_ref, split_ref, basis_ref, factor_ref, *, scale):
    columns = factor_ref.shape[0]
    width = 2 * columns
    scaled = factor_rows(unpack(parts_ref, columns) / scale, columns)
    lane = iota((columns, width), 1)
    sub = iota((columns, width), 0)
    factor_ref[...] = jnp.where(lane >= sub, scaled, 0.0)[:, :columns]
    right = jnp.where(lane >= columns, scaled, 0.0)
    twice = right + pltpu.roll(right, columns, 1)
    high = twice.astype(jnp.bfloat16)
    low = (twice - high.astype(jnp.float32)).astype(jnp.bfloat16)
    left = jnp.concatenate([high, low], axis=0)
    rows_y = basis_ref.shape[1] // columns
    cols_z = basis_ref.shape[2]
    for a in range(3):
        for y in range(0, rows_y, 2):
            wide = jnp.dot(
                left, split_ref[(a * rows_y + y) // 2], preferred_element_type=jnp.float32
            )
            wide = wide[:columns] + wide[columns:]
            for k in range(2):
                basis_ref[a, pl.ds(y + k, columns, stride=rows_y)] = wide[
                    :, k * cols_z : (k + 1) * cols_z
                ]


def vmem(count):
    return [pl.BlockSpec(memory_space=pltpu.VMEM)] * count


def params():
    return pltpu.CompilerParams(vmem_limit_bytes=VMEM_LIMIT)


def shards(coefficients, sketch):
    count = lax.axis_size("dom")
    coefs = coefficients[0]
    own = sketch[0]
    _, columns, rows_y, cols_z = own.shape
    chain = [(i, (i + 1) % count) for i in range(1, count, 2)]
    chain += [(b, a) for a, b in chain]
    chain_plane = lax.ppermute(own, "dom", chain)
    pairs = [(i, i ^ 1) for i in range(count)]
    pair_plane = lax.ppermute(own, "dom", pairs)
    part, far_coefs = pl.pallas_call(
        near_kernel,
        out_shape=(
            jax.ShapeDtypeStruct(own.shape, jnp.float32),
            jax.ShapeDtypeStruct((9, 3, 3, rows_y, cols_z), jnp.float32),
        ),
        in_specs=vmem(3),
        out_specs=tuple(vmem(2)),
        scratch_shapes=[pltpu.VMEM((18, 3, 3, rows_y, cols_z), jnp.float32)],
        compiler_params=params(),
        cost_estimate=pl.CostEstimate(
            flops=2 * 162 * own.size // 3, bytes_accessed=4 * own.size * 5, transcendentals=0
        ),
        name="near",
    )(coefs, own, pair_plane)
    packed = jax.ShapeDtypeStruct((1, 18 * columns), jnp.float32)
    split, mine, twin = pl.pallas_call(
        far_kernel,
        out_shape=(
            jax.ShapeDtypeStruct((3 * rows_y // 2, 2 * columns, 2 * cols_z), jnp.bfloat16),
            packed,
            packed,
        ),
        in_specs=vmem(3),
        out_specs=tuple(vmem(3)),
        scratch_shapes=[pltpu.VMEM((3, columns * rows_y, cols_z), jnp.float32)],
        compiler_params=params(),
        name="far",
    )(far_coefs, chain_plane, part)
    mine = mine + lax.ppermute(twin, "dom", pairs)
    parts = lax.all_to_all(jnp.broadcast_to(mine, (count,) + mine.shape), "dom", 0, 0)
    scale = 3.0 * count * rows_y * cols_z
    basis, factor = pl.pallas_call(
        functools.partial(basis_kernel, scale=scale),
        out_shape=(
            jax.ShapeDtypeStruct((3, columns * rows_y, cols_z), jnp.float32),
            jax.ShapeDtypeStruct((columns, columns), jnp.float32),
        ),
        in_specs=vmem(2),
        out_specs=tuple(vmem(2)),
        compiler_params=params(),
        name="basis",
    )(parts, split)
    return basis.reshape(sketch.shape), factor


def solution(mesh):
    placed = (P("dom", None, None, None, None, None), P("dom", None, None, None, None))
    return jax.shard_map(
        shards,
        mesh=mesh,
        in_specs=placed,
        out_specs=(P("dom", None, None, None, None), P()),
        check_vma=False,
    )
```

```python
import functools

import jax
import jax.numpy as jnp
from jax import lax
from jax.experimental import pallas as pl
from jax.experimental.pallas import tpu as pltpu
from jax.sharding import PartitionSpec as P

GROUP = 4
UNROLL = 8
VMEM_LIMIT = 48 * 1024 * 1024


def iota(shape, dim):
    return lax.broadcasted_iota(jnp.int32, shape, dim)


def side_bases():
    odd = lax.axis_index("dom") % 2
    return (1 - odd) * 18, odd * 18


def prepare(coef_ref, out_ref, base, first, keep):
    rows_y, cols_z = coef_ref.shape[3:]
    sub = iota((rows_y, cols_z), 0)
    lane = iota((rows_y, cols_z), 1)
    for dy in range(3):
        for dz in range(3):
            valid = None
            if dy == 0:
                valid = sub < rows_y - 1
            elif dy == 2:
                valid = sub > 0
            edge = None
            if dz == 0:
                edge = lane > 0
            elif dz == 2:
                edge = lane < cols_z - 1
            for a in range(3):
                for b in range(3):
                    block = coef_ref[base + dy * 3 + dz, a, b]
                    if dy == 0:
                        block = pltpu.roll(block, rows_y - 1, 0)
                    elif dy == 2:
                        block = pltpu.roll(block, 1, 0)
                    mask = valid
                    if edge is not None:
                        mask = edge if mask is None else mask & edge
                    if keep is not None:
                        mask = keep if mask is None else mask & keep
                    if mask is not None:
                        block = jnp.where(mask, block, 0.0)
                    out_ref[first + dy * 3 + dz, a, b] = block


def contract(coef_ref, parts, start, initial):
    rows_y, cols_z = coef_ref.shape[3:]
    zero = jnp.zeros((GROUP, rows_y, cols_z), jnp.float32)
    acc = [[zero for _ in range(3)] for _ in range(3)]
    for sketch_ref, slot, b, first in parts:
        own = sketch_ref[slot, pl.ds(start, GROUP)]
        for dz in range(3):
            moved = own
            if dz == 0:
                moved = pltpu.roll(own, 1, 2)
            elif dz == 2:
                moved = pltpu.roll(own, cols_z - 1, 2)
            for dy in range(3):
                for a in range(3):
                    acc[dy][a] += coef_ref[first + dy * 3 + dz, a, b][None] * moved
    out = []
    for a in range(3):
        total = acc[1][a] + pltpu.roll(acc[0][a], 1, 1) + pltpu.roll(acc[2][a], rows_y - 1, 1)
        if initial is not None:
            total = total + initial[a, pl.ds(start, GROUP)]
        out.append(total)
    return out


def near_kernel(coef_ref, own_ref, pair_ref, part_ref, far_coef_ref, work):
    pair_base, chain_base = side_bases()
    me = lax.axis_index("dom")
    count = lax.axis_size("dom")
    lone = (me == 0) | (me == count - 1)
    rows_y, cols_z = coef_ref.shape[3:]
    keep = iota((rows_y, cols_z), 0) >= jnp.where(lone, rows_y, 0)
    prepare(coef_ref, work, 9, 0, None)
    prepare(coef_ref, work, pair_base, 9, None)
    prepare(coef_ref, far_coef_ref, chain_base, 0, keep)
    parts = [(own_ref, b, b, 0) for b in range(3)] + [(pair_ref, b, b, 9) for b in range(3)]

    def step(i, carry):
        start = i * GROUP
        out = contract(work, parts, start, None)
        for a in range(3):
            part_ref[a, pl.ds(start, GROUP)] = out[a]
        return carry

    lax.fori_loop(0, own_ref.shape[1] // GROUP, step, 0, unroll=UNROLL)


def pack(gram, half, columns):
    quarter = columns // 4
    width = 2 * columns
    lane = iota((quarter, width), 1) % columns
    sub = iota((quarter, width), 0)
    base = half * 2 * quarter
    first = pltpu.roll(gram[base : base + quarter], (width - base) % width, 1)
    second = pltpu.roll(gram[base + quarter : base + 2 * quarter], width - base - quarter, 1)
    cross = gram[half * quarter : (half + 1) * quarter]
    packed = jnp.where(
        (lane < quarter) & (lane < sub), second, jnp.where(lane < 2 * quarter, first, cross)
    )
    last = jnp.sum(jnp.where(lane == sub, second, 0.0), axis=0, keepdims=True)
    wide = iota((8, width), 1)
    return [jnp.where(wide < columns, packed[:8], packed[8:]), last]


def far_kernel(far_coef_ref, chain_ref, part_ref, split_ref, mine_ref, twin_ref, work):
    columns = chain_ref.shape[1]
    rows_y, cols_z = chain_ref.shape[2:]
    parts = [(chain_ref, b, b, 0) for b in range(3)]

    def step(i, carry):
        start = i * GROUP
        out = contract(far_coef_ref, parts, start, part_ref)
        for a in range(3):
            work[a, pl.ds(start * rows_y, GROUP * rows_y)] = out[a].reshape(
                GROUP * rows_y, cols_z
            )
        return carry

    lax.fori_loop(0, columns // GROUP, step, 0, unroll=UNROLL)
    total = jnp.zeros((2 * columns, 2 * columns), jnp.float32)
    for a in range(3):
        for y in range(0, rows_y, 2):
            both = []
            for yy in (y, y + 1):
                x = work[a, pl.ds(yy, columns, stride=rows_y)]
                high = x.astype(jnp.bfloat16)
                low = (x - high.astype(jnp.float32)).astype(jnp.bfloat16)
                both.append(jnp.concatenate([high, low], axis=0))
            wide = jnp.concatenate(both, axis=1)
            split_ref[(a * rows_y + y) // 2] = wide
            total += lax.dot_general(
                wide, wide, (((1,), (1,)), ((), ())), preferred_element_type=jnp.float32
            )
    rows = total[:columns] + total[columns:]
    gram = rows + pltpu.roll(rows, columns, 1)
    odd = lax.axis_index("dom") % 2 == 1
    halves = [pack(gram, h, columns) for h in range(2)]
    for ref, flip in ((mine_ref, False), (twin_ref, True)):
        low, high = halves[::-1] if flip else halves
        body = jnp.where(odd, high[0], low[0])
        for r in range(8):
            ref[:, r * 2 * columns : (r + 1) * 2 * columns] = body[r : r + 1]
        ref[:, 16 * columns :] = jnp.where(odd, high[1], low[1])


def unpack(parts_ref, columns):
    width = 2 * columns
    quarter = columns // 4
    sub8 = iota((8, width), 0)
    rows = []
    for r in range(9):
        x = parts_ref[:, 0, r * width : (r + 1) * width]
        x = jnp.sum(x.reshape(2, x.shape[0] // 16, 8, width), axis=1)
        x = jnp.where(sub8 < 4, x[0] + pltpu.roll(x[0], 4, 0), x[1] + pltpu.roll(x[1], 4, 0))
        x = x + pltpu.roll(x, 2, 0)
        rows.append(x + pltpu.roll(x, 1, 0))
    lane = iota((quarter, width), 1)
    sub = iota((quarter, width), 0)
    out = []
    for half in range(2):
        at = 4 * half + 3
        body = jnp.zeros((8, width), jnp.float32)
        for r in range(8):
            body = jnp.where(
                sub8 == r, jnp.broadcast_to(rows[r][at : at + 1], (8, width)), body
            )
        packed = jnp.concatenate([body, pltpu.roll(body, columns, 1)], axis=0)
        base = half * 2 * quarter
        upper = jnp.where(lane >= sub, packed, 0.0)
        upper = jnp.where(lane < 2 * quarter, upper, 0.0)
        lower = jnp.where(lane < sub, packed, 0.0)
        diag = jnp.broadcast_to(rows[8][at : at + 1], (quarter, width))
        lower = jnp.where(lane == sub, diag, lower)
        lower = jnp.where(lane < quarter, lower, 0.0)
        cross = jnp.where((lane >= 2 * quarter) & (lane < columns), packed, 0.0)
        if base:
            upper = pltpu.roll(upper, base, 1)
        out.append((upper, pltpu.roll(lower, base + quarter, 1), cross))
    once = jnp.concatenate(
        [out[0][0] + out[0][2], out[0][1] + out[1][2], out[1][0], out[1][1]], axis=0
    )
    lane = iota((columns, width), 1)
    sub = iota((columns, width), 0)
    square = jnp.concatenate([once, jnp.zeros_like(once)], axis=0)
    mirror = jnp.transpose(square)[:columns]
    return once + jnp.where(lane == sub, 0.0, mirror)


def factor_rows(gram, columns):
    lane = iota(gram.shape, 1)
    sub = iota(gram.shape, 0)
    both = jnp.where(lane - columns == sub, 1.0, gram)
    count = columns // 8
    shape = (8, 2 * columns)
    blocks = [both[8 * j : 8 * j + 8] for j in range(count)]
    sub8 = iota(shape, 0)
    def spread(block, column):
        return jnp.broadcast_to(block[:, column : column + 1], shape)

    def repeat(block, row):
        return jnp.broadcast_to(block[row : row + 1], shape)

    done = []
    ahead = [spread(blocks[0], c) for c in range(8)]
    for j in range(count):
        own = ahead
        mine = blocks[j]
        rest = range(j + 1, count)
        if j + 1 < count:
            ahead = [spread(blocks[j + 1], 8 * (j + 1) + c) for c in range(8)]
        panel = {r: [spread(blocks[r], 8 * j + c) for c in range(8)] for r in rest}
        pivots = None
        for i in range(8):
            heads = {c: repeat(own[c], i) for c in range(i, 8)}
            row = repeat(mine, i)
            inverse = 1.0 / heads[i]
            pivots = heads[i] if i == 0 else jnp.where(sub8 == i, heads[i], pivots)
            if i < 7:
                scale = jnp.where(sub8 > i, own[i] * inverse, 0.0)
                for c in range(i + 1, 8):
                    if c == i + 1:
                        product = jnp.where(sub8 > i, own[i] * heads[c], 0.0)
                        own[c] = own[c] - product * inverse
                    else:
                        own[c] = own[c] - scale * heads[c]
                mine = mine - scale * row
            for r in rest:
                scale = panel[r][i] * inverse
                if r == j + 1:
                    for c in range(8):
                        ahead[c] = ahead[c] - scale * repeat(panel[r][i], c)
                for c in range(i + 1, 8):
                    panel[r][c] = panel[r][c] - scale * heads[c]
                blocks[r] = blocks[r] - scale * row
        done.append(mine * (1.0 / jnp.sqrt(pivots)))
    return jnp.concatenate(done, axis=0)


def basis_kernel(parts_ref, split_ref, basis_ref, factor_ref, *, scale):
    columns = factor_ref.shape[0]
    width = 2 * columns
    scaled = factor_rows(unpack(parts_ref, columns) / scale, columns)
    lane = iota((columns, width), 1)
    sub = iota((columns, width), 0)
    factor_ref[...] = jnp.where(lane >= sub, scaled, 0.0)[:, :columns]
    right = jnp.where(lane >= columns, scaled, 0.0)
    twice = right + pltpu.roll(right, columns, 1)
    high = twice.astype(jnp.bfloat16)
    low = (twice - high.astype(jnp.float32)).astype(jnp.bfloat16)
    left = jnp.concatenate([high, low], axis=0)
    rows_y = basis_ref.shape[1] // columns
    cols_z = basis_ref.shape[2]
    for a in range(3):
        for y in range(0, rows_y, 2):
            wide = jnp.dot(
                left, split_ref[(a * rows_y + y) // 2], preferred_element_type=jnp.float32
            )
            wide = wide[:columns] + wide[columns:]
            for k in range(2):
                basis_ref[a, pl.ds(y + k, columns, stride=rows_y)] = wide[
                    :, k * cols_z : (k + 1) * cols_z
                ]


def vmem(count):
    return [pl.BlockSpec(memory_space=pltpu.VMEM)] * count


def params():
    return pltpu.CompilerParams(vmem_limit_bytes=VMEM_LIMIT)


def shards(coefficients, sketch):
    count = lax.axis_size("dom")
    coefs = coefficients[0]
    own = sketch[0]
    _, columns, rows_y, cols_z = own.shape
    chain = [(i, (i + 1) % count) for i in range(1, count, 2)]
    chain += [(b, a) for a, b in chain]
    chain_plane = lax.ppermute(own, "dom", chain)
    pairs = [(i, i ^ 1) for i in range(count)]
    pair_plane = lax.ppermute(own, "dom", pairs)
    part, far_coefs = pl.pallas_call(
        near_kernel,
        out_shape=(
            jax.ShapeDtypeStruct(own.shape, jnp.float32),
            jax.ShapeDtypeStruct((9, 3, 3, rows_y, cols_z), jnp.float32),
        ),
        in_specs=vmem(3),
        out_specs=tuple(vmem(2)),
        scratch_shapes=[pltpu.VMEM((18, 3, 3, rows_y, cols_z), jnp.float32)],
        compiler_params=params(),
        cost_estimate=pl.CostEstimate(
            flops=2 * 162 * own.size // 3, bytes_accessed=4 * own.size * 5, transcendentals=0
        ),
        name="near",
    )(coefs, own, pair_plane)
    packed = jax.ShapeDtypeStruct((1, 18 * columns), jnp.float32)
    split, mine, twin = pl.pallas_call(
        far_kernel,
        out_shape=(
            jax.ShapeDtypeStruct((3 * rows_y // 2, 2 * columns, 2 * cols_z), jnp.bfloat16),
            packed,
            packed,
        ),
        in_specs=vmem(3),
        out_specs=tuple(vmem(3)),
        scratch_shapes=[pltpu.VMEM((3, columns * rows_y, cols_z), jnp.float32)],
        compiler_params=params(),
        name="far",
    )(far_coefs, chain_plane, part)
    mine = mine + lax.ppermute(twin, "dom", pairs)
    order = [*range(0, count, 2), *range(1, count, 2)]
    parts = lax.all_to_all(
        jnp.broadcast_to(mine, (count,) + mine.shape), "dom", 0, 0, axis_index_groups=[order]
    )
    scale = 3.0 * count * rows_y * cols_z
    basis, factor = pl.pallas_call(
        functools.partial(basis_kernel, scale=scale),
        out_shape=(
            jax.ShapeDtypeStruct((3, columns * rows_y, cols_z), jnp.float32),
            jax.ShapeDtypeStruct((columns, columns), jnp.float32),
        ),
        in_specs=vmem(2),
        out_specs=tuple(vmem(2)),
        compiler_params=params(),
        name="basis",
    )(parts, split)
    return basis.reshape(sketch.shape), factor


def solution(mesh):
    placed = (P("dom", None, None, None, None, None), P("dom", None, None, None, None))
    return jax.shard_map(
        shards,
        mesh=mesh,
        in_specs=placed,
        out_specs=(P("dom", None, None, None, None), P()),
        check_vma=False,
    )
```

```python
import functools

import jax
import jax.numpy as jnp
from jax import lax
from jax.experimental import pallas as pl
from jax.experimental.pallas import tpu as pltpu
from jax.sharding import PartitionSpec as P

GROUP = 4
UNROLL = 8
VMEM_LIMIT = 48 * 1024 * 1024


def iota(shape, dim):
    return lax.broadcasted_iota(jnp.int32, shape, dim)


def side_bases():
    odd = lax.axis_index("dom") % 2
    return (1 - odd) * 18, odd * 18


def prepare(coef_ref, out_ref, base, first, keep):
    rows_y, cols_z = coef_ref.shape[3:]
    sub = iota((rows_y, cols_z), 0)
    lane = iota((rows_y, cols_z), 1)
    for dy in range(3):
        for dz in range(3):
            valid = None
            if dy == 0:
                valid = sub < rows_y - 1
            elif dy == 2:
                valid = sub > 0
            edge = None
            if dz == 0:
                edge = lane > 0
            elif dz == 2:
                edge = lane < cols_z - 1
            for a in range(3):
                for b in range(3):
                    block = coef_ref[base + dy * 3 + dz, a, b]
                    if dy == 0:
                        block = pltpu.roll(block, rows_y - 1, 0)
                    elif dy == 2:
                        block = pltpu.roll(block, 1, 0)
                    mask = valid
                    if edge is not None:
                        mask = edge if mask is None else mask & edge
                    if keep is not None:
                        mask = keep if mask is None else mask & keep
                    if mask is not None:
                        block = jnp.where(mask, block, 0.0)
                    out_ref[first + dy * 3 + dz, a, b] = block


def contract(coef_ref, parts, start, initial):
    rows_y, cols_z = coef_ref.shape[3:]
    acc = [[None] * 3, [None] * 3, [None] * 3]
    if initial is not None:
        acc[1] = [initial[a, pl.ds(start, GROUP)] for a in range(3)]
    for sketch_ref, slot, b, first in parts:
        own = sketch_ref[slot, pl.ds(start, GROUP)]
        for dz in range(3):
            moved = own
            if dz == 0:
                moved = pltpu.roll(own, 1, 2)
            elif dz == 2:
                moved = pltpu.roll(own, cols_z - 1, 2)
            for dy in range(3):
                for a in range(3):
                    term = coef_ref[first + dy * 3 + dz, a, b][None] * moved
                    acc[dy][a] = term if acc[dy][a] is None else acc[dy][a] + term
    return [
        acc[1][a] + pltpu.roll(acc[0][a], 1, 1) + pltpu.roll(acc[2][a], rows_y - 1, 1)
        for a in range(3)
    ]


def near_kernel(coef_ref, own_ref, pair_ref, part_ref, far_coef_ref, work):
    pair_base, chain_base = side_bases()
    me = lax.axis_index("dom")
    count = lax.axis_size("dom")
    lone = (me == 0) | (me == count - 1)
    rows_y, cols_z = coef_ref.shape[3:]
    keep = iota((rows_y, cols_z), 0) >= jnp.where(lone, rows_y, 0)
    prepare(coef_ref, work, 9, 0, None)
    prepare(coef_ref, work, pair_base, 9, None)
    prepare(coef_ref, far_coef_ref, chain_base, 0, keep)
    parts = [(own_ref, b, b, 0) for b in range(3)] + [(pair_ref, b, b, 9) for b in range(3)]

    def step(i, carry):
        start = i * GROUP
        out = contract(work, parts, start, None)
        for a in range(3):
            part_ref[a, pl.ds(start, GROUP)] = out[a]
        return carry

    lax.fori_loop(0, own_ref.shape[1] // GROUP, step, 0, unroll=UNROLL)


def pack(gram, half, columns):
    quarter = columns // 4
    width = 2 * columns
    lane = iota((quarter, width), 1) % columns
    sub = iota((quarter, width), 0)
    base = half * 2 * quarter
    first = pltpu.roll(gram[base : base + quarter], (width - base) % width, 1)
    second = pltpu.roll(gram[base + quarter : base + 2 * quarter], width - base - quarter, 1)
    cross = gram[half * quarter : (half + 1) * quarter]
    packed = jnp.where(
        (lane < quarter) & (lane < sub), second, jnp.where(lane < 2 * quarter, first, cross)
    )
    last = jnp.sum(jnp.where(lane == sub, second, 0.0), axis=0, keepdims=True)
    wide = iota((8, width), 1)
    return [jnp.where(wide < columns, packed[:8], packed[8:]), last]


def far_kernel(far_coef_ref, chain_ref, part_ref, split_ref, mine_ref, twin_ref, work):
    columns = chain_ref.shape[1]
    rows_y, cols_z = chain_ref.shape[2:]
    parts = [(chain_ref, b, b, 0) for b in range(3)]

    def step(i, carry):
        start = i * GROUP
        out = contract(far_coef_ref, parts, start, part_ref)
        for a in range(3):
            work[a, pl.ds(start * rows_y, GROUP * rows_y)] = out[a].reshape(
                GROUP * rows_y, cols_z
            )
        return carry

    lax.fori_loop(0, columns // GROUP, step, 0, unroll=UNROLL)
    total = jnp.zeros((2 * columns, 2 * columns), jnp.float32)
    for a in range(3):
        for y in range(0, rows_y, 2):
            both = []
            for yy in (y, y + 1):
                x = work[a, pl.ds(yy, columns, stride=rows_y)]
                high = x.astype(jnp.bfloat16)
                low = (x - high.astype(jnp.float32)).astype(jnp.bfloat16)
                both.append(jnp.concatenate([high, low], axis=0))
            wide = jnp.concatenate(both, axis=1)
            split_ref[(a * rows_y + y) // 2] = wide
            total += lax.dot_general(
                wide, wide, (((1,), (1,)), ((), ())), preferred_element_type=jnp.float32
            )
    rows = total[:columns] + total[columns:]
    gram = rows + pltpu.roll(rows, columns, 1)
    odd = lax.axis_index("dom") % 2 == 1
    halves = [pack(gram, h, columns) for h in range(2)]
    for ref, flip in ((mine_ref, False), (twin_ref, True)):
        low, high = halves[::-1] if flip else halves
        body = jnp.where(odd, high[0], low[0])
        for r in range(8):
            ref[:, r * 2 * columns : (r + 1) * 2 * columns] = body[r : r + 1]
        ref[:, 16 * columns :] = jnp.where(odd, high[1], low[1])


def unpack(parts_ref, columns):
    width = 2 * columns
    quarter = columns // 4
    sub8 = iota((8, width), 0)
    rows = []
    for r in range(9):
        x = parts_ref[:, 0, r * width : (r + 1) * width]
        x = jnp.sum(x.reshape(2, x.shape[0] // 16, 8, width), axis=1)
        x = jnp.where(sub8 < 4, x[0] + pltpu.roll(x[0], 4, 0), x[1] + pltpu.roll(x[1], 4, 0))
        x = x + pltpu.roll(x, 2, 0)
        rows.append(x + pltpu.roll(x, 1, 0))
    lane = iota((quarter, width), 1)
    sub = iota((quarter, width), 0)
    out = []
    for half in range(2):
        at = 4 * half + 3
        body = jnp.zeros((8, width), jnp.float32)
        for r in range(8):
            body = jnp.where(
                sub8 == r, jnp.broadcast_to(rows[r][at : at + 1], (8, width)), body
            )
        packed = jnp.concatenate([body, pltpu.roll(body, columns, 1)], axis=0)
        base = half * 2 * quarter
        upper = jnp.where(lane >= sub, packed, 0.0)
        upper = jnp.where(lane < 2 * quarter, upper, 0.0)
        lower = jnp.where(lane < sub, packed, 0.0)
        diag = jnp.broadcast_to(rows[8][at : at + 1], (quarter, width))
        lower = jnp.where(lane == sub, diag, lower)
        lower = jnp.where(lane < quarter, lower, 0.0)
        cross = jnp.where((lane >= 2 * quarter) & (lane < columns), packed, 0.0)
        if base:
            upper = pltpu.roll(upper, base, 1)
        out.append((upper, pltpu.roll(lower, base + quarter, 1), cross))
    once = jnp.concatenate(
        [out[0][0] + out[0][2], out[0][1] + out[1][2], out[1][0], out[1][1]], axis=0
    )
    lane = iota((columns, width), 1)
    sub = iota((columns, width), 0)
    square = jnp.concatenate([once, jnp.zeros_like(once)], axis=0)
    mirror = jnp.transpose(square)[:columns]
    return once + jnp.where(lane == sub, 0.0, mirror)


def factor_rows(gram, columns):
    lane = iota(gram.shape, 1)
    sub = iota(gram.shape, 0)
    both = jnp.where(lane - columns == sub, 1.0, gram)
    count = columns // 8
    shape = (8, 2 * columns)
    blocks = [both[8 * j : 8 * j + 8] for j in range(count)]
    sub8 = iota(shape, 0)
    def spread(block, column):
        return jnp.broadcast_to(block[:, column : column + 1], shape)

    def repeat(block, row):
        return jnp.broadcast_to(block[row : row + 1], shape)

    done = []
    ahead = [spread(blocks[0], c) for c in range(8)]
    for j in range(count):
        own = ahead
        mine = blocks[j]
        rest = range(j + 1, count)
        if j + 1 < count:
            ahead = [spread(blocks[j + 1], 8 * (j + 1) + c) for c in range(8)]
        panel = {r: [spread(blocks[r], 8 * j + c) for c in range(8)] for r in rest}
        pivots = None
        for i in range(8):
            heads = {c: repeat(own[c], i) for c in range(i, 8)}
            row = repeat(mine, i)
            inverse = 1.0 / heads[i]
            pivots = heads[i] if i == 0 else jnp.where(sub8 == i, heads[i], pivots)
            if i < 7:
                scale = jnp.where(sub8 > i, own[i] * inverse, 0.0)
                for c in range(i + 1, 8):
                    if c == i + 1:
                        product = jnp.where(sub8 > i, own[i] * heads[c], 0.0)
                        own[c] = own[c] - product * inverse
                    else:
                        own[c] = own[c] - scale * heads[c]
                mine = mine - scale * row
            for r in rest:
                scale = panel[r][i] * inverse
                if r == j + 1:
                    for c in range(8):
                        ahead[c] = ahead[c] - scale * repeat(panel[r][i], c)
                for c in range(i + 1, 8):
                    panel[r][c] = panel[r][c] - scale * heads[c]
                blocks[r] = blocks[r] - scale * row
        done.append(mine * (1.0 / jnp.sqrt(pivots)))
    return jnp.concatenate(done, axis=0)


def basis_kernel(parts_ref, split_ref, basis_ref, factor_ref, *, scale):
    columns = factor_ref.shape[0]
    width = 2 * columns
    scaled = factor_rows(unpack(parts_ref, columns) / scale, columns)
    lane = iota((columns, width), 1)
    sub = iota((columns, width), 0)
    factor_ref[...] = jnp.where(lane >= sub, scaled, 0.0)[:, :columns]
    right = jnp.where(lane >= columns, scaled, 0.0)
    twice = right + pltpu.roll(right, columns, 1)
    high = twice.astype(jnp.bfloat16)
    low = (twice - high.astype(jnp.float32)).astype(jnp.bfloat16)
    left = jnp.concatenate([high, low], axis=0)
    rows_y = basis_ref.shape[1] // columns
    cols_z = basis_ref.shape[2]
    for a in range(3):
        for y in range(0, rows_y, 2):
            wide = jnp.dot(
                left, split_ref[(a * rows_y + y) // 2], preferred_element_type=jnp.float32
            )
            wide = wide[:columns] + wide[columns:]
            for k in range(2):
                basis_ref[a, pl.ds(y + k, columns, stride=rows_y)] = wide[
                    :, k * cols_z : (k + 1) * cols_z
                ]


def vmem(count):
    return [pl.BlockSpec(memory_space=pltpu.VMEM)] * count


def params():
    return pltpu.CompilerParams(vmem_limit_bytes=VMEM_LIMIT)


def shards(coefficients, sketch):
    count = lax.axis_size("dom")
    coefs = coefficients[0]
    own = sketch[0]
    _, columns, rows_y, cols_z = own.shape
    chain = [(i, (i + 1) % count) for i in range(1, count, 2)]
    chain += [(b, a) for a, b in chain]
    chain_plane = lax.ppermute(own, "dom", chain)
    pairs = [(i, i ^ 1) for i in range(count)]
    pair_plane = lax.ppermute(own, "dom", pairs)
    part, far_coefs = pl.pallas_call(
        near_kernel,
        out_shape=(
            jax.ShapeDtypeStruct(own.shape, jnp.float32),
            jax.ShapeDtypeStruct((9, 3, 3, rows_y, cols_z), jnp.float32),
        ),
        in_specs=vmem(3),
        out_specs=tuple(vmem(2)),
        scratch_shapes=[pltpu.VMEM((18, 3, 3, rows_y, cols_z), jnp.float32)],
        compiler_params=params(),
        cost_estimate=pl.CostEstimate(
            flops=2 * 162 * own.size // 3, bytes_accessed=4 * own.size * 5, transcendentals=0
        ),
        name="near",
    )(coefs, own, pair_plane)
    packed = jax.ShapeDtypeStruct((1, 18 * columns), jnp.float32)
    split, mine, twin = pl.pallas_call(
        far_kernel,
        out_shape=(
            jax.ShapeDtypeStruct((3 * rows_y // 2, 2 * columns, 2 * cols_z), jnp.bfloat16),
            packed,
            packed,
        ),
        in_specs=vmem(3),
        out_specs=tuple(vmem(3)),
        scratch_shapes=[pltpu.VMEM((3, columns * rows_y, cols_z), jnp.float32)],
        compiler_params=params(),
        name="far",
    )(far_coefs, chain_plane, part)
    mine = mine + lax.ppermute(twin, "dom", pairs)
    order = [*range(count // 2, count, 2), *range(0, count // 2, 2), *range(count // 2 + 1, count, 2), *range(1, count // 2, 2)]
    parts = lax.all_to_all(
        jnp.broadcast_to(mine, (count,) + mine.shape), "dom", 0, 0, axis_index_groups=[order]
    )
    scale = 3.0 * count * rows_y * cols_z
    basis, factor = pl.pallas_call(
        functools.partial(basis_kernel, scale=scale),
        out_shape=(
            jax.ShapeDtypeStruct((3, columns * rows_y, cols_z), jnp.float32),
            jax.ShapeDtypeStruct((columns, columns), jnp.float32),
        ),
        in_specs=vmem(2),
        out_specs=tuple(vmem(2)),
        compiler_params=params(),
        name="basis",
    )(parts, split)
    return basis.reshape(sketch.shape), factor


def solution(mesh):
    placed = (P("dom", None, None, None, None, None), P("dom", None, None, None, None))
    return jax.shard_map(
        shards,
        mesh=mesh,
        in_specs=placed,
        out_specs=(P("dom", None, None, None, None), P()),
        check_vma=False,
    )
```

```python
import functools

import jax
import jax.numpy as jnp
from jax import lax
from jax.experimental import pallas as pl
from jax.experimental.pallas import tpu as pltpu
from jax.sharding import PartitionSpec as P

GROUP = 2
UNROLL = 16
VMEM_LIMIT = 48 * 1024 * 1024


def iota(shape, dim):
    return lax.broadcasted_iota(jnp.int32, shape, dim)


def side_bases():
    odd = lax.axis_index("dom") % 2
    return (1 - odd) * 18, odd * 18


def prepare(coef_ref, out_ref, base, first, keep):
    rows_y, cols_z = coef_ref.shape[3:]
    sub = iota((rows_y, cols_z), 0)
    lane = iota((rows_y, cols_z), 1)
    for dy in range(3):
        for dz in range(3):
            valid = None
            if dy == 0:
                valid = sub < rows_y - 1
            elif dy == 2:
                valid = sub > 0
            edge = None
            if dz == 0:
                edge = lane > 0
            elif dz == 2:
                edge = lane < cols_z - 1
            for a in range(3):
                for b in range(3):
                    block = coef_ref[base + dy * 3 + dz, a, b]
                    if dy == 0:
                        block = pltpu.roll(block, rows_y - 1, 0)
                    elif dy == 2:
                        block = pltpu.roll(block, 1, 0)
                    mask = valid
                    if edge is not None:
                        mask = edge if mask is None else mask & edge
                    if keep is not None:
                        mask = keep if mask is None else mask & keep
                    if mask is not None:
                        block = jnp.where(mask, block, 0.0)
                    out_ref[first + dy * 3 + dz, a, b] = block


def contract(coef_ref, parts, start, initial):
    rows_y, cols_z = coef_ref.shape[3:]
    acc = [[None] * 3, [None] * 3, [None] * 3]
    if initial is not None:
        acc[1] = [initial[a, pl.ds(start, GROUP)] for a in range(3)]
    for sketch_ref, slot, b, first in parts:
        own = sketch_ref[slot, pl.ds(start, GROUP)]
        for dz in range(3):
            moved = own
            if dz == 0:
                moved = pltpu.roll(own, 1, 2)
            elif dz == 2:
                moved = pltpu.roll(own, cols_z - 1, 2)
            for dy in range(3):
                for a in range(3):
                    term = coef_ref[first + dy * 3 + dz, a, b][None] * moved
                    acc[dy][a] = term if acc[dy][a] is None else acc[dy][a] + term
    return [
        acc[1][a] + pltpu.roll(acc[0][a], 1, 1) + pltpu.roll(acc[2][a], rows_y - 1, 1)
        for a in range(3)
    ]


def near_kernel(coef_ref, own_ref, pair_ref, part_ref, far_coef_ref, work):
    pair_base, chain_base = side_bases()
    me = lax.axis_index("dom")
    count = lax.axis_size("dom")
    lone = (me == 0) | (me == count - 1)
    rows_y, cols_z = coef_ref.shape[3:]
    keep = iota((rows_y, cols_z), 0) >= jnp.where(lone, rows_y, 0)
    prepare(coef_ref, work, 9, 0, None)
    prepare(coef_ref, work, pair_base, 9, None)
    prepare(coef_ref, far_coef_ref, chain_base, 0, keep)
    parts = [(own_ref, b, b, 0) for b in range(3)] + [(pair_ref, b, b, 9) for b in range(3)]

    def step(i, carry):
        start = i * GROUP
        out = contract(work, parts, start, None)
        for a in range(3):
            part_ref[a, pl.ds(start, GROUP)] = out[a]
        return carry

    lax.fori_loop(0, own_ref.shape[1] // GROUP, step, 0, unroll=UNROLL)


def pack(gram, half, columns):
    quarter = columns // 4
    width = 2 * columns
    lane = iota((quarter, width), 1) % columns
    sub = iota((quarter, width), 0)
    base = half * 2 * quarter
    first = pltpu.roll(gram[base : base + quarter], (width - base) % width, 1)
    second = pltpu.roll(gram[base + quarter : base + 2 * quarter], width - base - quarter, 1)
    cross = gram[half * quarter : (half + 1) * quarter]
    packed = jnp.where(
        (lane < quarter) & (lane < sub), second, jnp.where(lane < 2 * quarter, first, cross)
    )
    last = jnp.sum(jnp.where(lane == sub, second, 0.0), axis=0, keepdims=True)
    wide = iota((8, width), 1)
    return [jnp.where(wide < columns, packed[:8], packed[8:]), last]


def far_kernel(far_coef_ref, chain_ref, part_ref, split_ref, mine_ref, twin_ref, work):
    columns = chain_ref.shape[1]
    rows_y, cols_z = chain_ref.shape[2:]
    parts = [(chain_ref, b, b, 0) for b in range(3)]

    def step(i, carry):
        start = i * GROUP
        out = contract(far_coef_ref, parts, start, part_ref)
        for a in range(3):
            work[a, pl.ds(start * rows_y, GROUP * rows_y)] = out[a].reshape(
                GROUP * rows_y, cols_z
            )
        return carry

    lax.fori_loop(0, columns // GROUP, step, 0, unroll=UNROLL)
    total = jnp.zeros((2 * columns, 2 * columns), jnp.float32)
    for a in range(3):
        for y in range(0, rows_y, 2):
            both = []
            for yy in (y, y + 1):
                x = work[a, pl.ds(yy, columns, stride=rows_y)]
                high = x.astype(jnp.bfloat16)
                low = (x - high.astype(jnp.float32)).astype(jnp.bfloat16)
                both.append(jnp.concatenate([high, low], axis=0))
            wide = jnp.concatenate(both, axis=1)
            split_ref[(a * rows_y + y) // 2] = wide
            total += lax.dot_general(
                wide, wide, (((1,), (1,)), ((), ())), preferred_element_type=jnp.float32
            )
    rows = total[:columns] + total[columns:]
    gram = rows + pltpu.roll(rows, columns, 1)
    odd = lax.axis_index("dom") % 2 == 1
    halves = [pack(gram, h, columns) for h in range(2)]
    for ref, flip in ((mine_ref, False), (twin_ref, True)):
        low, high = halves[::-1] if flip else halves
        body = jnp.where(odd, high[0], low[0])
        for r in range(8):
            ref[:, r * 2 * columns : (r + 1) * 2 * columns] = body[r : r + 1]
        ref[:, 16 * columns :] = jnp.where(odd, high[1], low[1])


def unpack(parts_ref, columns):
    width = 2 * columns
    quarter = columns // 4
    sub8 = iota((8, width), 0)
    rows = []
    for r in range(9):
        x = parts_ref[:, 0, r * width : (r + 1) * width]
        x = jnp.sum(x.reshape(2, x.shape[0] // 16, 8, width), axis=1)
        x = jnp.where(sub8 < 4, x[0] + pltpu.roll(x[0], 4, 0), x[1] + pltpu.roll(x[1], 4, 0))
        x = x + pltpu.roll(x, 2, 0)
        rows.append(x + pltpu.roll(x, 1, 0))
    lane = iota((quarter, width), 1)
    sub = iota((quarter, width), 0)
    out = []
    for half in range(2):
        at = 4 * half + 3
        body = jnp.zeros((8, width), jnp.float32)
        for r in range(8):
            body = jnp.where(
                sub8 == r, jnp.broadcast_to(rows[r][at : at + 1], (8, width)), body
            )
        packed = jnp.concatenate([body, pltpu.roll(body, columns, 1)], axis=0)
        base = half * 2 * quarter
        upper = jnp.where(lane >= sub, packed, 0.0)
        upper = jnp.where(lane < 2 * quarter, upper, 0.0)
        lower = jnp.where(lane < sub, packed, 0.0)
        diag = jnp.broadcast_to(rows[8][at : at + 1], (quarter, width))
        lower = jnp.where(lane == sub, diag, lower)
        lower = jnp.where(lane < quarter, lower, 0.0)
        cross = jnp.where((lane >= 2 * quarter) & (lane < columns), packed, 0.0)
        if base:
            upper = pltpu.roll(upper, base, 1)
        out.append((upper, pltpu.roll(lower, base + quarter, 1), cross))
    once = jnp.concatenate(
        [out[0][0] + out[0][2], out[0][1] + out[1][2], out[1][0], out[1][1]], axis=0
    )
    lane = iota((columns, width), 1)
    sub = iota((columns, width), 0)
    square = jnp.concatenate([once, jnp.zeros_like(once)], axis=0)
    mirror = jnp.transpose(square)[:columns]
    return once + jnp.where(lane == sub, 0.0, mirror)


def factor_rows(gram, columns):
    lane = iota(gram.shape, 1)
    sub = iota(gram.shape, 0)
    both = jnp.where(lane - columns == sub, 1.0, gram)
    count = columns // 8
    shape = (8, 2 * columns)
    blocks = [both[8 * j : 8 * j + 8] for j in range(count)]
    sub8 = iota(shape, 0)
    def spread(block, column):
        return jnp.broadcast_to(block[:, column : column + 1], shape)

    def repeat(block, row):
        return jnp.broadcast_to(block[row : row + 1], shape)

    done = []
    ahead = [spread(blocks[0], c) for c in range(8)]
    for j in range(count):
        own = ahead
        mine = blocks[j]
        rest = range(j + 1, count)
        if j + 1 < count:
            ahead = [spread(blocks[j + 1], 8 * (j + 1) + c) for c in range(8)]
        panel = {r: [spread(blocks[r], 8 * j + c) for c in range(8)] for r in rest}
        pivots = None
        for i in range(8):
            heads = {c: repeat(own[c], i) for c in range(i, 8)}
            row = repeat(mine, i)
            inverse = 1.0 / heads[i]
            pivots = heads[i] if i == 0 else jnp.where(sub8 == i, heads[i], pivots)
            if i < 7:
                scale = jnp.where(sub8 > i, own[i] * inverse, 0.0)
                for c in range(i + 1, 8):
                    if c == i + 1:
                        product = jnp.where(sub8 > i, own[i] * heads[c], 0.0)
                        own[c] = own[c] - product * inverse
                    else:
                        own[c] = own[c] - scale * heads[c]
                mine = mine - scale * row
            for r in rest:
                scale = panel[r][i] * inverse
                if r == j + 1:
                    for c in range(8):
                        ahead[c] = ahead[c] - scale * repeat(panel[r][i], c)
                for c in range(i + 1, 8):
                    panel[r][c] = panel[r][c] - scale * heads[c]
                blocks[r] = blocks[r] - scale * row
        done.append(mine * (1.0 / jnp.sqrt(pivots)))
    return jnp.concatenate(done, axis=0)


def basis_kernel(parts_ref, split_ref, basis_ref, factor_ref, *, scale):
    columns = factor_ref.shape[0]
    width = 2 * columns
    scaled = factor_rows(unpack(parts_ref, columns) / scale, columns)
    lane = iota((columns, width), 1)
    sub = iota((columns, width), 0)
    factor_ref[...] = jnp.where(lane >= sub, scaled, 0.0)[:, :columns]
    right = jnp.where(lane >= columns, scaled, 0.0)
    twice = right + pltpu.roll(right, columns, 1)
    high = twice.astype(jnp.bfloat16)
    low = (twice - high.astype(jnp.float32)).astype(jnp.bfloat16)
    left = jnp.concatenate([high, low], axis=0)
    rows_y = basis_ref.shape[1] // columns
    cols_z = basis_ref.shape[2]
    for a in range(3):
        for y in range(0, rows_y, 2):
            wide = jnp.dot(
                left, split_ref[(a * rows_y + y) // 2], preferred_element_type=jnp.float32
            )
            wide = wide[:columns] + wide[columns:]
            for k in range(2):
                basis_ref[a, pl.ds(y + k, columns, stride=rows_y)] = wide[
                    :, k * cols_z : (k + 1) * cols_z
                ]


def vmem(count):
    return [pl.BlockSpec(memory_space=pltpu.VMEM)] * count


def params():
    return pltpu.CompilerParams(vmem_limit_bytes=VMEM_LIMIT)


def shards(coefficients, sketch):
    count = lax.axis_size("dom")
    coefs = coefficients[0]
    own = sketch[0]
    _, columns, rows_y, cols_z = own.shape
    chain = [(i, (i + 1) % count) for i in range(1, count, 2)]
    chain += [(b, a) for a, b in chain]
    chain_plane = lax.ppermute(own, "dom", chain)
    pairs = [(i, i ^ 1) for i in range(count)]
    pair_plane = lax.ppermute(own, "dom", pairs)
    part, far_coefs = pl.pallas_call(
        near_kernel,
        out_shape=(
            jax.ShapeDtypeStruct(own.shape, jnp.float32),
            jax.ShapeDtypeStruct((9, 3, 3, rows_y, cols_z), jnp.float32),
        ),
        in_specs=vmem(3),
        out_specs=tuple(vmem(2)),
        scratch_shapes=[pltpu.VMEM((18, 3, 3, rows_y, cols_z), jnp.float32)],
        compiler_params=params(),
        cost_estimate=pl.CostEstimate(
            flops=2 * 162 * own.size // 3, bytes_accessed=4 * own.size * 5, transcendentals=0
        ),
        name="near",
    )(coefs, own, pair_plane)
    packed = jax.ShapeDtypeStruct((1, 18 * columns), jnp.float32)
    split, mine, twin = pl.pallas_call(
        far_kernel,
        out_shape=(
            jax.ShapeDtypeStruct((3 * rows_y // 2, 2 * columns, 2 * cols_z), jnp.bfloat16),
            packed,
            packed,
        ),
        in_specs=vmem(3),
        out_specs=tuple(vmem(3)),
        scratch_shapes=[pltpu.VMEM((3, columns * rows_y, cols_z), jnp.float32)],
        compiler_params=params(),
        name="far",
    )(far_coefs, chain_plane, part)
    mine = mine + lax.ppermute(twin, "dom", pairs)
    order = [*range(count // 2, count, 2), *range(0, count // 2, 2), *range(count // 2 + 1, count, 2), *range(1, count // 2, 2)]
    parts = lax.all_to_all(
        jnp.broadcast_to(mine, (count,) + mine.shape), "dom", 0, 0, axis_index_groups=[order]
    )
    scale = 3.0 * count * rows_y * cols_z
    basis, factor = pl.pallas_call(
        functools.partial(basis_kernel, scale=scale),
        out_shape=(
            jax.ShapeDtypeStruct((3, columns * rows_y, cols_z), jnp.float32),
            jax.ShapeDtypeStruct((columns, columns), jnp.float32),
        ),
        in_specs=vmem(2),
        out_specs=tuple(vmem(2)),
        compiler_params=params(),
        name="basis",
    )(parts, split)
    return basis.reshape(sketch.shape), factor


def solution(mesh):
    placed = (P("dom", None, None, None, None, None), P("dom", None, None, None, None))
    return jax.shard_map(
        shards,
        mesh=mesh,
        in_specs=placed,
        out_specs=(P("dom", None, None, None, None), P()),
        check_vma=False,
    )
```
